512 devices in a mesh: row: 32 (over x, y, core), col: 16 (over z).
Axes of the slice: x: 4, y: 4, z: 16, core: 2. Of those that a mesh axis runs over, the one named last changes fastest.
Arguments:
- momentum: bfloat16 [8192, 28672], P('row', 'col'), may hold values from -120 to 120
- gradient: bfloat16 [8192, 28672], P('row', 'col'), may hold values from -6 to 6
- right_factor: bfloat16 [28672, 256], P('col'), may hold values from -0.03125 to 0.03125
Outputs:
- new_momentum: bfloat16 [8192, 28672], P('row', 'col')
- new_right: bfloat16 [28672, 256], P('col')
- left_factor: float32 [8192, 256], P('row')
The draws below stay inside these ranges and needn't reach their ends.
All inputs are finite; a program needn't handle non-finite values.
Results may differ from the reference program's by a relative error of at most 0.013.
Values sent between devices are 32-bit elements; how exact they have to be, the bound alone decides.
No kernel may reach another device: no remote copies, remote signals or barrier semaphores. Data moves between devices by JAX's collectives and lax.ppermute only.
A program may use at most 64 MiB of HBM per device.

```python
import math
import jax
import jax.numpy as jnp
from jax import lax

D = 8192
FF = 28672
RANK = 256


def draw_momentum(key, part):
    key = jax.random.fold_in(key, 7)
    first, second, third, fourth, fifth = jax.random.split(key, 5)
    spread = RANK // 8
    left_ints = jax.random.randint(fourth, (D, spread), -7, 8, jnp.int32)
    right_ints = jax.random.randint(fifth, (spread, FF), -7, 8, jnp.int32)
    shared = jnp.dot(left_ints, right_ints).astype(jnp.float32) * (3.0 / (56.0 * math.sqrt(spread)))
    row_log = jax.random.uniform(first, (D, 1), jnp.float32, 0.0, math.log(10.0))
    values = jax.random.normal(third, (D, FF), jnp.float32)
    level = 0.1
    col_log = jax.random.uniform(second, (1, FF), jnp.float32, 0.0, math.log(10.0))
    trend = 1.0 + 2.0 * jnp.arange(FF, dtype=jnp.float32)[None, :] / (FF - 1)
    combined = jnp.clip(0.95 * shared + 0.3 * values, -4.0, 4.0)
    return (level * combined * jnp.exp(row_log) * jnp.exp(col_log) * trend).astype(jnp.bfloat16)


def levels(own_key, extent, cuts, low, high):
    def one(dim, shards_of):
        draws = jax.random.uniform(jax.random.fold_in(jax.random.fold_in(own_key, 6), dim), (shards_of,), jnp.float32, low / len(cuts), high / len(cuts))
        return jnp.repeat(jnp.exp(draws), extent[dim] // shards_of).reshape((-1,) + (1,) * (len(extent) - dim - 1))

    level = one(*cuts[0])
    for cut in cuts[1:]:
        level = level * one(*cut)
    return level


def gaussian(stream_key, dims, width, reach, shards=(), held_as=jnp.bfloat16):
    entries = width * jax.random.normal(stream_key, dims, jnp.float32)
    if shards:
        entries = entries * levels(stream_key, dims, shards, -0.22, 0.18)
    return jnp.clip(entries, -reach, reach).astype(held_as)


def setup_inputs(seed: int = 0) -> dict:
    splits = jax.random.split(jax.random.key(seed), 4)
    return {
        "momentum": draw_momentum(jax.random.fold_in(splits[3], 71), 0),
        "gradient": gaussian(splits[1], (D, FF), 1.0, 6.0, ((0, 32), (1, 16))),
        "right_factor": gaussian(splits[2], (FF, RANK), FF ** -0.5, 0.03125, ((0, 16),)),
    }


def reference(momentum, gradient, right_factor):
    blend = (momentum.astype(jnp.float32) + gradient.astype(jnp.float32)).astype(jnp.bfloat16)
    left = jnp.dot(blend.astype(jnp.float32), right_factor.astype(jnp.float32), preferred_element_type=jnp.float32)
    gram = jnp.dot(left.T, left, precision=lax.Precision.HIGHEST)
    lower = jnp.linalg.cholesky(gram)
    left_factor = lax.linalg.triangular_solve(lower, left, left_side=False, lower=True, transpose_a=True)
    ortho_b = left_factor.astype(jnp.bfloat16)
    right = lax.dot_general(blend.astype(jnp.float32), ortho_b.astype(jnp.float32), (((0,), (0,)), ((), ())), preferred_element_type=jnp.float32)
    total = lax.optimization_barrier(jnp.sum(right * right, axis=0))
    new_right = (right * lax.rsqrt(total + 1e-08)).astype(jnp.bfloat16)
    right_b = right.astype(jnp.bfloat16)
    correction = lax.dot_general(ortho_b.astype(jnp.float32), right_b.astype(jnp.float32), (((1,), (1,)), ((), ())), preferred_element_type=jnp.float32)
    new_momentum = (blend.astype(jnp.float32) - 0.1 * correction).astype(jnp.bfloat16)
    return (new_momentum, new_right, left_factor)
```

```python
import jax
import jax.numpy as jnp
from jax import lax
from jax.sharding import PartitionSpec as P

ROWS = 32
COLS = 16
HIGHEST = lax.Precision.HIGHEST
SAME_CORE = [[2 * chip + core for chip in range(ROWS // 2)] for core in range(2)]
SIBLINGS = [(index, index ^ 1) for index in range(ROWS)]


def scatter_sum(x, axis, count, groups=None):
    moved = lax.all_to_all(x, axis, 0, 0, axis_index_groups=groups, tiled=True)
    return jnp.sum(moved.reshape(count, x.shape[0] // count, x.shape[1]), axis=0)


def gather(x, axis, count, groups=None):
    copies = jnp.broadcast_to(x[None], (count,) + x.shape).reshape(count * x.shape[0], x.shape[1])
    return lax.all_to_all(copies, axis, 0, 0, axis_index_groups=groups, tiled=True)


def split3(x):
    first = lax.reduce_precision(x, 8, 7)
    rest = x - first
    second = lax.reduce_precision(rest, 8, 7)
    third = rest - second
    return first.astype(jnp.bfloat16), second.astype(jnp.bfloat16), third.astype(jnp.bfloat16)


def row_sum_large(x):
    core = lax.axis_index("row") % 2
    half = x.shape[0] // 2
    other = lax.dynamic_slice_in_dim(x, (1 - core) * half, half, 0)
    mine = lax.dynamic_slice_in_dim(x, core * half, half, 0)
    mine = mine + lax.ppermute(other, "row", SIBLINGS)
    piece = scatter_sum(mine, "row", ROWS // 2, SAME_CORE)
    mine = gather(piece, "row", ROWS // 2, SAME_CORE)
    other = lax.ppermute(mine, "row", SIBLINGS)
    first = jnp.where(core == 0, mine, other)
    second = jnp.where(core == 0, other, mine)
    return jnp.concatenate([first, second], axis=0)


def local(momentum, gradient, right_factor):
    blend = (momentum.astype(jnp.float32) + gradient.astype(jnp.float32)).astype(jnp.bfloat16)
    left = jnp.dot(blend, right_factor, preferred_element_type=jnp.float32)
    left = gather(scatter_sum(left, "col", COLS), "col", COLS)
    gram = jnp.dot(left.T, left, precision=HIGHEST)
    gram = gather(scatter_sum(gram, "row", ROWS), "row", ROWS)
    product = sum(
        lax.dot_general(blend, term, (((0,), (0,)), ((), ())), preferred_element_type=jnp.float32)
        for term in split3(left)
    )
    product = row_sum_large(product)
    lower = jnp.linalg.cholesky(gram)
    inverse = lax.linalg.triangular_solve(lower, jnp.eye(gram.shape[0], dtype=jnp.float32), left_side=True, lower=True)
    left_factor = jnp.dot(left, inverse.T, precision=HIGHEST)
    right = jnp.dot(product, inverse.T, precision=HIGHEST)
    ortho_b = left_factor.astype(jnp.bfloat16)
    sums = jnp.sum(right * right, axis=0, keepdims=True)
    total = jnp.sum(gather(sums, "col", COLS), axis=0)
    new_right = (right * lax.rsqrt(total + 1e-08)).astype(jnp.bfloat16)
    right_b = right.astype(jnp.bfloat16)
    correction = lax.dot_general(
        ortho_b, right_b, (((1,), (1,)), ((), ())), preferred_element_type=jnp.float32
    )
    new_momentum = (blend.astype(jnp.float32) - 0.1 * correction).astype(jnp.bfloat16)
    return (new_momentum, new_right, left_factor)


def solution(mesh):
    placed = (P("row", "col"), P("row", "col"), P("col", None))
    return jax.shard_map(
        local,
        mesh=mesh,
        in_specs=placed,
        out_specs=(P("row", "col"), P("col", None), P("row", None)),
        check_vma=False,
    )
```

```python
import functools
import jax
import jax.numpy as jnp
from jax import lax
from jax.experimental import pallas as pl
from jax.experimental.pallas import tpu as pltpu
from jax.sharding import Mesh, PartitionSpec as P

HIGHEST = lax.Precision.HIGHEST
VMEM = pl.BlockSpec(memory_space=pltpu.VMEM)


def scatter_sum(x, axis, count):
    moved = lax.all_to_all(x, axis, 0, 0, tiled=True)
    return jnp.sum(moved.reshape(count, x.shape[0] // count, x.shape[1]), axis=0)


def gather(x, axis, count):
    copies = jnp.broadcast_to(x[None], (count,) + x.shape).reshape(count * x.shape[0], x.shape[1])
    return lax.all_to_all(copies, axis, 0, 0, tiled=True)


def nt(a, b):
    return lax.dot_general(a, b, (((1,), (1,)), ((), ())), precision=HIGHEST, preferred_element_type=jnp.float32)

def factor_block(block):
    size = block.shape[0]
    rest = block
    done = []
    for start in range(0, size, 8):
        height = size - start
        row = lax.broadcasted_iota(jnp.int32, (height, 128), 0)
        cols = [jnp.broadcast_to(rest[:, start + m:start + m + 1], (height, 128)) for m in range(8)]
        tile = rest[:8]
        pivots = jnp.ones((8, 128), jnp.float32)
        gains = []
        for m in range(8):
            pivot = cols[m][m:m + 1]
            gain = jnp.where(row > m, cols[m] * (1.0 / pivot), 0.0)
            for q in range(m + 1, 8):
                cols[q] = cols[q] - gain * cols[q][m:m + 1]
            tile = tile - gain[:8] * tile[m:m + 1]
            pivots = jnp.where(row[:8] == m, pivot, pivots)
            gains.append(gain)
        done.append(tile * lax.rsqrt(pivots))
        if height > 8:
            rest = rest[8:]
            for m in range(8):
                rest = rest - gains[m][8:] * tile[m:m + 1]
    return jnp.concatenate(done, axis=0)

def inverse_factor_kernel(size, core_ref, mine_ref, other_ref, out_ref, a_ref, y_ref):
    n = out_ref.shape[0]
    first = core_ref[0] == 0
    mine = mine_ref[...].reshape(n // 2, n)
    other = other_ref[...].reshape(n // 2, n)
    a_ref[:n // 2, :] = jnp.where(first, mine, other)
    a_ref[n // 2:, :] = jnp.where(first, other, mine)
    r = lax.broadcasted_iota(jnp.int32, (n, n), 0)
    c = lax.broadcasted_iota(jnp.int32, (n, n), 1)
    y_ref[...] = jnp.where(r == c, 1.0, 0.0)
    r = lax.broadcasted_iota(jnp.int32, (size, 128), 0)
    c = lax.broadcasted_iota(jnp.int32, (size, 128), 1)
    for o in range(0, n, size):
        end = o + size
        base = o // 128 * 128
        diag = a_ref[o:end, base:base + 128]
        if o % 128:
            diag = pltpu.roll(diag, 128 - o % 128, 1)
        block = jnp.where(c < size, diag, jnp.where(c - size == r, 1.0, 0.0))
        small = factor_block(block)
        inverse = small[:, size:2 * size]
        value = jnp.dot(inverse, y_ref[o:end, :], precision=HIGHEST, preferred_element_type=jnp.float32)
        out_ref[o:end, :] = value
        if end < n:
            panel = nt(a_ref[end:, o:end], inverse)
            a_ref[end:, :] = a_ref[end:, :] - jnp.concatenate([jnp.zeros((n - end, end), jnp.float32), nt(panel, panel)], axis=1)
            y_ref[end:, :] = y_ref[end:, :] - jnp.dot(panel, value, precision=HIGHEST, preferred_element_type=jnp.float32)

def inverse_factor(core, mine, other, size=64):
    pieces, height, n = mine.shape
    small = n // 2 // pieces
    spec = pl.BlockSpec((pieces, small, n), lambda step: (0, height // small - 1, 0))
    return pl.pallas_call(
        functools.partial(inverse_factor_kernel, size),
        grid=(1,),
        out_shape=jax.ShapeDtypeStruct((n, n), jnp.float32),
        in_specs=[pl.BlockSpec(memory_space=pltpu.SMEM), spec, spec],
        out_specs=pl.BlockSpec((n, n), lambda step: (0, 0)),
        scratch_shapes=[pltpu.VMEM((n, n), jnp.float32), pltpu.VMEM((n, n), jnp.float32)],
        name="inverse_factor",
    )(core, mine, other)


def sum_copies_kernel(in_ref, out_ref):
    count = in_ref.shape[0]
    total = in_ref[0]
    for index in range(1, count):
        total = total + in_ref[index]
    for index in range(count):
        out_ref[index] = total


def sum_copies(parts):
    return pl.pallas_call(
        sum_copies_kernel,
        out_shape=jax.ShapeDtypeStruct(parts.shape, parts.dtype),
        in_specs=[VMEM],
        out_specs=VMEM,
        name="sum_copies",
    )(parts)


def right_kernel(core_ref, mine_ref, other_ref, inverse_ref, right_ref, sums_ref):
    chips, height, rank = mine_ref.shape
    swap = core_ref[0] != pl.program_id(0)
    rows = jnp.where(swap, other_ref[...], mine_ref[...]).reshape(chips * height, rank)
    right = nt(rows, inverse_ref[...])
    right_ref[...] = right
    sums = jnp.sum(right * right, axis=0, keepdims=True)

    @pl.when((pl.program_id(0) == 0) & (pl.program_id(1) == 0))
    def _():
        sums_ref[...] = sums

    @pl.when((pl.program_id(0) != 0) | (pl.program_id(1) != 0))
    def _():
        sums_ref[...] += sums


def right_and_sums(core, mine, other, inverse, steps=2):
    pieces, height, rank = mine.shape
    large = height - rank // 2 // pieces
    chips = pieces // steps
    spec = pl.BlockSpec((chips, large, rank), lambda half, step: (step, 0, 0))
    return pl.pallas_call(
        right_kernel,
        grid=(2, steps),
        out_shape=(
            jax.ShapeDtypeStruct((2 * pieces * large, rank), jnp.float32),
            jax.ShapeDtypeStruct((1, rank), jnp.float32),
        ),
        in_specs=[
            pl.BlockSpec(memory_space=pltpu.SMEM), spec, spec,
            pl.BlockSpec((rank, rank), lambda half, step: (0, 0)),
        ],
        out_specs=(
            pl.BlockSpec((chips * large, rank), lambda half, step: (half * steps + step, 0)),
            pl.BlockSpec((1, rank), lambda half, step: (0, 0)),
        ),
        name="right_and_sums",
    )(core, mine, other, inverse)


def feedback_kernel(left_ref, inverse_ref, right_ref, blend_ref, momentum_ref, factor_ref):
    factor = nt(left_ref[...], inverse_ref[...])
    factor_ref[...] = factor
    ortho = factor.astype(jnp.bfloat16)
    width = blend_ref.shape[1]
    tile = width // 2
    for at in range(0, width, tile):
        correction = lax.dot_general(
            ortho, right_ref[at:at + tile, :].astype(jnp.bfloat16), (((1,), (1,)), ((), ())),
            preferred_element_type=jnp.float32,
        )
        blend = blend_ref[:, at:at + tile].astype(jnp.float32)
        momentum_ref[:, at:at + tile] = (blend - 0.1 * correction).astype(jnp.bfloat16)


def feedback(left, inverse, right, blend):
    return pl.pallas_call(
        feedback_kernel,
        out_shape=(jax.ShapeDtypeStruct(blend.shape, blend.dtype), jax.ShapeDtypeStruct(left.shape, jnp.float32)),
        in_specs=[VMEM] * 4,
        out_specs=(VMEM, VMEM),
        compiler_params=pltpu.CompilerParams(vmem_limit_bytes=32 * 1024 * 1024),
        name="feedback",
    )(left, inverse, right, blend)


def products_kernel(pieces, left_ref, blend_ref, out_ref):
    left = left_ref[...]
    rank = left.shape[1]
    gram = lax.dot_general(left, left, (((0,), (0,)), ((), ())), precision=HIGHEST, preferred_element_type=jnp.float32)
    first = left.astype(jnp.bfloat16)
    rest = left - first.astype(jnp.float32)
    second = rest.astype(jnp.bfloat16)
    third = (rest - second.astype(jnp.float32)).astype(jnp.bfloat16)
    terms = jnp.concatenate([first, second, third], axis=1)
    wide = blend_ref.shape[1]
    large, small = wide // pieces, rank // pieces
    piece = large + small
    for part in range(2):
        half = wide // 2
        both = lax.dot_general(
            blend_ref[:, part * half:(part + 1) * half], terms, (((0,), (0,)), ((), ())),
            preferred_element_type=jnp.float32,
        )
        product = both[:, :rank] + both[:, rank:2 * rank] + both[:, 2 * rank:]
        for index in range(pieces // 2):
            at = (part * (pieces // 2) + index) * piece
            out_ref[at:at + large, :] = product[index * large:(index + 1) * large]
    for index in range(pieces):
        at = index * piece + large
        out_ref[at:at + small, :] = gram[index * small:(index + 1) * small]


def products(left, blend, pieces):
    return pl.pallas_call(
        functools.partial(products_kernel, pieces),
        out_shape=jax.ShapeDtypeStruct((blend.shape[1] + left.shape[1], left.shape[1]), jnp.float32),
        in_specs=[VMEM, VMEM],
        out_specs=VMEM,
        compiler_params=pltpu.CompilerParams(vmem_limit_bytes=32 * 1024 * 1024),
        name="products",
    )(left, blend)


def local(chips, cores, cols, momentum, gradient, right_factor):
    blend = (momentum.astype(jnp.float32) + gradient.astype(jnp.float32)).astype(jnp.bfloat16)
    left = jnp.dot(blend, right_factor, preferred_element_type=jnp.float32)
    left = gather(scatter_sum(left, "col", cols), "col", cols)

    both = products(left, blend, chips * cores)
    both = scatter_sum(both, "core", cores)
    both = lax.all_to_all(both.reshape(chips, -1, both.shape[1]), "chip", 0, 0)
    mine = lax.all_to_all(sum_copies(both), "chip", 0, 0)
    other = lax.ppermute(mine, "core", [(0, 1), (1, 0)])
    core = lax.axis_index("core").astype(jnp.int32).reshape(1)
    inverse = inverse_factor(core, mine, other)
    right, sums = right_and_sums(core, mine, other, inverse)
    total = jnp.sum(gather(sums, "col", cols), axis=0)
    new_momentum, left_factor = feedback(left, inverse, right, blend)
    new_right = (right * lax.rsqrt(total + 1e-08)).astype(jnp.bfloat16)
    return (new_momentum, new_right, left_factor)


def solution(mesh):
    rows, cols = mesh.devices.shape
    chips, cores = rows // 2, 2
    split = Mesh(mesh.devices.reshape(chips, cores, cols), ("chip", "core", "col"))
    row = ("chip", "core")
    placed = (P(row, "col"), P(row, "col"), P("col", None))
    return jax.shard_map(
        functools.partial(local, chips, cores, cols),
        mesh=split,
        in_specs=placed,
        out_specs=(P(row, "col"), P("col", None), P(row, None)),
        check_vma=False,
    )
```

```python
import functools
import jax
import jax.numpy as jnp
from jax import lax
from jax.experimental import pallas as pl
from jax.experimental.pallas import tpu as pltpu
from jax.sharding import Mesh, PartitionSpec as P

HIGHEST = lax.Precision.HIGHEST
VMEM = pl.BlockSpec(memory_space=pltpu.VMEM)


def scatter_sum(x, axis, count):
    moved = lax.all_to_all(x, axis, 0, 0, tiled=True)
    return jnp.sum(moved.reshape(count, x.shape[0] // count, x.shape[1]), axis=0)


def gather(x, axis, count):
    copies = jnp.broadcast_to(x[None], (count,) + x.shape).reshape(count * x.shape[0], x.shape[1])
    return lax.all_to_all(copies, axis, 0, 0, tiled=True)


def nt(a, b):
    return lax.dot_general(a, b, (((1,), (1,)), ((), ())), precision=HIGHEST, preferred_element_type=jnp.float32)


def nn(a, b):
    return lax.dot_general(a, b, (((1,), (0,)), ((), ())), precision=HIGHEST, preferred_element_type=jnp.float32)


def factor_block(block, panel):
    size = block.shape[0]
    rest = block
    done = []
    for start in range(0, size, panel):
        height = size - start
        row = lax.broadcasted_iota(jnp.int32, (height, 128), 0)
        cols = [jnp.broadcast_to(rest[:, start + m:start + m + 1], (height, 128)) for m in range(panel)]
        tile = rest[:panel]
        pivots = jnp.ones((panel, 128), jnp.float32)
        gains = []
        for m in range(0, panel, 2):
            top = cols[m][m:m + 1]
            side = cols[m + 1][m:m + 1]
            low = cols[m + 1][m + 1:m + 2]
            det = top * low - side * side
            rtop = 1.0 / top
            rlow = top * (1.0 / det)
            slope = side * rtop
            g0 = jnp.where(row > m, cols[m] * rtop, 0.0)
            nxt = cols[m + 1] - g0 * side
            g1 = jnp.where(row > m + 1, nxt * rlow, 0.0)
            for q in range(m + 2, panel):
                u = cols[q][m:m + 1]
                v = cols[q][m + 1:m + 2] - slope * u
                cols[q] = (cols[q] - g0 * u) - g1 * v
            tile = tile - g0[:panel] * tile[m:m + 1]
            tile = tile - g1[:panel] * tile[m + 1:m + 2]
            pivots = jnp.where(row[:panel] == m, top, jnp.where(row[:panel] == m + 1, det * rtop, pivots))
            gains += [g0, g1]
        done.append(tile * lax.rsqrt(pivots))
        if height > panel:
            rest = rest[panel:]
            for m in range(panel):
                rest = rest - gains[m][panel:] * tile[m:m + 1]
    return jnp.concatenate(done, axis=0)


def inverse_factor_kernel(size, panel, mine_ref, out_ref, a_ref, y_ref):
    n = out_ref.shape[0]
    pieces, height, _ = mine_ref.shape
    r = lax.broadcasted_iota(jnp.int32, (n, n), 0)
    c = lax.broadcasted_iota(jnp.int32, (n, n), 1)
    gram = mine_ref[:, height - n // pieces:, :].reshape(n, n)
    diagonal = jnp.where(r == c, gram, 0.0)
    across = lax.rsqrt(jnp.sum(diagonal, axis=0, keepdims=True))
    down = lax.rsqrt(jnp.sum(diagonal, axis=1, keepdims=True))
    a_ref[...] = gram * across * down
    y_ref[...] = jnp.where(r == c, across, 0.0)
    count = n // size
    a = {}
    for i in range(count):
        for j in range(i + 1):
            a[i, j] = a_ref[i * size:(i + 1) * size, j * size:(j + 1) * size]
    eye = jnp.where(r[:size, :size] == c[:size, :size], 1.0, 0.0)
    y = [y_ref[i * size:(i + 1) * size, :] for i in range(count)]
    for k in range(count):
        small = factor_block(jnp.concatenate([a[k, k], eye], axis=1), panel)
        inverse = small[:, size:2 * size]
        p = {}
        for i in range(k + 1, count):
            p[i] = nt(a[i, k], inverse)
            for j in range(k + 1, i + 1):
                a[i, j] = a[i, j] - nt(p[i], p[j])
        lim = ((k + 1) * size + 127) // 128 * 128
        value = nn(inverse, y[k][:, :lim])
        out_ref[k * size:(k + 1) * size, :lim] = value
        if lim < n:
            out_ref[k * size:(k + 1) * size, lim:] = jnp.zeros((size, n - lim), jnp.float32)
        for i in range(k + 1, count):
            left = y[i][:, :lim] - nn(p[i], value)
            y[i] = left if lim == n else jnp.concatenate([left, y[i][:, lim:]], axis=1)


def inverse_factor(mine, size=64, panel=16):
    n = mine.shape[2]
    return pl.pallas_call(
        functools.partial(inverse_factor_kernel, size, panel),
        out_shape=jax.ShapeDtypeStruct((n, n), jnp.float32),
        in_specs=[VMEM],
        out_specs=VMEM,
        scratch_shapes=[pltpu.VMEM((n, n), jnp.float32), pltpu.VMEM((n, n), jnp.float32)],
        compiler_params=pltpu.CompilerParams(vmem_limit_bytes=8 * 1024 * 1024),
        name="inverse_factor",
    )(mine)


def sum_copies_kernel(in_ref, out_ref):
    count = in_ref.shape[0]
    total = in_ref[0]
    for index in range(1, count):
        total = total + in_ref[index]
    for index in range(count):
        out_ref[index] = total


def sum_copies(parts):
    return pl.pallas_call(
        sum_copies_kernel,
        out_shape=jax.ShapeDtypeStruct(parts.shape, parts.dtype),
        in_specs=[VMEM],
        out_specs=VMEM,
        compiler_params=pltpu.CompilerParams(vmem_limit_bytes=8 * 1024 * 1024),
        name="sum_copies",
    )(parts)


def right_kernel(mine_ref, inverse_ref, right_ref, sums_ref):
    pieces, height, rank = mine_ref.shape
    large = right_ref.shape[0] // pieces
    rows = mine_ref[:, :large, :].reshape(pieces * large, rank)
    right = nt(rows, inverse_ref[...])
    right_ref[...] = right
    sums_ref[...] = jnp.broadcast_to(jnp.sum(right * right, axis=0)[None, None], sums_ref.shape)


def right_and_sums(mine, inverse, count):
    pieces, height, rank = mine.shape
    large = height - rank // pieces
    return pl.pallas_call(
        right_kernel,
        out_shape=(
            jax.ShapeDtypeStruct((pieces * large, rank), jnp.float32),
            jax.ShapeDtypeStruct((count, 1, rank), jnp.float32),
        ),
        in_specs=[VMEM, VMEM],
        out_specs=(VMEM, VMEM),
        compiler_params=pltpu.CompilerParams(vmem_limit_bytes=10 * 1024 * 1024),
        name="right_and_sums",
    )(mine, inverse)


def sum_pair_kernel(in_ref, out_ref):
    out_ref[...] = in_ref[0] + in_ref[1]


def sum_pair(parts):
    return pl.pallas_call(
        sum_pair_kernel,
        out_shape=jax.ShapeDtypeStruct(parts.shape[1:], parts.dtype),
        in_specs=[VMEM],
        out_specs=VMEM,
        compiler_params=pltpu.CompilerParams(vmem_limit_bytes=8 * 1024 * 1024),
        name="sum_pair",
    )(parts)


def feedback_kernel(core_ref, left_ref, inverse_ref, mine_ref, other_ref, blend_ref, momentum_ref, factor_ref):
    factor = nt(left_ref[...], inverse_ref[...])
    factor_ref[...] = factor
    ortho = factor.astype(jnp.bfloat16)
    half = mine_ref.shape[0]
    for part in range(2):
        right = jnp.where(core_ref[0] == part, mine_ref[...], other_ref[...])
        correction = lax.dot_general(
            ortho, right.astype(jnp.bfloat16), (((1,), (1,)), ((), ())), preferred_element_type=jnp.float32
        )
        at = part * half
        blend = blend_ref[:, at:at + half].astype(jnp.float32)
        momentum_ref[:, at:at + half] = (blend - 0.1 * correction).astype(jnp.bfloat16)


def feedback(core, left, inverse, mine, other, blend):
    return pl.pallas_call(
        feedback_kernel,
        out_shape=(jax.ShapeDtypeStruct(blend.shape, blend.dtype), jax.ShapeDtypeStruct(left.shape, jnp.float32)),
        in_specs=[pl.BlockSpec(memory_space=pltpu.SMEM)] + [VMEM] * 5,
        out_specs=(VMEM, VMEM),
        compiler_params=pltpu.CompilerParams(vmem_limit_bytes=12 * 1024 * 1024),
        cost_estimate=pl.CostEstimate(flops=0, bytes_accessed=0, transcendentals=0),
        name="feedback",
    )(core, left, inverse, mine, other, blend)


def normalize_kernel(core_ref, mine_ref, other_ref, sums_ref, out_ref):
    scale = lax.rsqrt(jnp.sum(sums_ref[...], axis=0) + 1e-08)
    half = mine_ref.shape[0]
    for part in range(2):
        right = jnp.where(core_ref[0] == part, mine_ref[...], other_ref[...])
        out_ref[part * half:(part + 1) * half, :] = (right * scale).astype(jnp.bfloat16)


def normalize(core, mine, other, sums):
    rows, rank = mine.shape
    return pl.pallas_call(
        normalize_kernel,
        out_shape=jax.ShapeDtypeStruct((2 * rows, rank), jnp.bfloat16),
        in_specs=[pl.BlockSpec(memory_space=pltpu.SMEM)] + [VMEM] * 3,
        out_specs=VMEM,
        compiler_params=pltpu.CompilerParams(vmem_limit_bytes=8 * 1024 * 1024),
        name="normalize",
    )(core, mine, other, sums)


def products_kernel(left_ref, blend_ref, out_ref):
    left = left_ref[...]
    rank = left.shape[1]
    cores, chips = out_ref.shape[:2]
    gram = lax.dot_general(left, left, (((0,), (0,)), ((), ())), precision=HIGHEST, preferred_element_type=jnp.float32)
    first = left.astype(jnp.bfloat16)
    rest = left - first.astype(jnp.float32)
    second = rest.astype(jnp.bfloat16)
    third = (rest - second.astype(jnp.float32)).astype(jnp.bfloat16)
    terms = jnp.concatenate([first, second, third], axis=1)
    half = blend_ref.shape[1] // cores
    large, small = half // chips, rank // chips
    for core in range(cores):
        both = lax.dot_general(
            blend_ref[:, core * half:(core + 1) * half], terms, (((0,), (0,)), ((), ())),
            preferred_element_type=jnp.float32,
        )
        product = both[:, :rank] + both[:, rank:2 * rank] + both[:, 2 * rank:]
        for chip in range(chips):
            out_ref[core, chip, :large, :] = product[chip * large:(chip + 1) * large]
            out_ref[core, chip, large:, :] = gram[chip * small:(chip + 1) * small]


def products(left, blend, cores, chips):
    rank = left.shape[1]
    height = blend.shape[1] // cores // chips + rank // chips
    return pl.pallas_call(
        products_kernel,
        out_shape=jax.ShapeDtypeStruct((cores, chips, height, rank), jnp.float32),
        in_specs=[VMEM, VMEM],
        out_specs=VMEM,
        compiler_params=pltpu.CompilerParams(vmem_limit_bytes=12 * 1024 * 1024),
        name="products",
    )(left, blend)


def local(chips, cores, cols, momentum, gradient, right_factor):
    blend = (momentum.astype(jnp.float32) + gradient.astype(jnp.float32)).astype(jnp.bfloat16)
    left = jnp.dot(blend, right_factor, preferred_element_type=jnp.float32)
    left = gather(scatter_sum(left, "col", cols), "col", cols)

    both = sum_pair(lax.all_to_all(products(left, blend, cores, chips), "core", 0, 0))
    mine = lax.all_to_all(sum_copies(lax.all_to_all(both, "chip", 0, 0)), "chip", 0, 0)
    inverse = inverse_factor(mine)
    swap = [(0, 1), (1, 0)]
    core = lax.axis_index("core").astype(jnp.int32).reshape(1)
    right, sums = right_and_sums(mine, inverse, cores * cols)
    sums = lax.all_to_all(sums, ("core", "col"), 0, 0)
    other = lax.ppermute(right, "core", swap)
    new_momentum, left_factor = feedback(core, left, inverse, right, other, blend)
    new_right = normalize(core, right, other, sums)
    return (new_momentum, new_right, left_factor)


def solution(mesh):
    rows, cols = mesh.devices.shape
    chips, cores = rows // 2, 2
    split = Mesh(mesh.devices.reshape(chips, cores, cols), ("chip", "core", "col"))
    row = ("chip", "core")
    placed = (P(row, "col"), P(row, "col"), P("col", None))
    return jax.shard_map(
        functools.partial(local, chips, cores, cols),
        mesh=split,
        in_specs=placed,
        out_specs=(P(row, "col"), P("col", None), P(row, None)),
        check_vma=False,
    )
```

```python
import functools
import jax
import jax.numpy as jnp
from jax import lax
from jax.experimental import pallas as pl
from jax.experimental.pallas import tpu as pltpu
from jax.sharding import Mesh, PartitionSpec as P

HIGHEST = lax.Precision.HIGHEST
VMEM = pl.BlockSpec(memory_space=pltpu.VMEM)


def nt(a, b):
    return lax.dot_general(a, b, (((1,), (1,)), ((), ())), precision=HIGHEST, preferred_element_type=jnp.float32)


def nn(a, b):
    return lax.dot_general(a, b, (((1,), (0,)), ((), ())), precision=HIGHEST, preferred_element_type=jnp.float32)


def factor_block(block, panel):
    size = block.shape[0]
    rest = block
    done = []
    for start in range(0, size, panel):
        height = size - start
        row = lax.broadcasted_iota(jnp.int32, (height, 128), 0)
        cols = [jnp.broadcast_to(rest[:, start + m:start + m + 1], (height, 128)) for m in range(panel)]
        tile = rest[:panel]
        pivots = jnp.ones((panel, 128), jnp.float32)
        gains = []
        for m in range(0, panel, 2):
            top = cols[m][m:m + 1]
            side = cols[m + 1][m:m + 1]
            low = cols[m + 1][m + 1:m + 2]
            det = top * low - side * side
            rtop = 1.0 / top
            rlow = top * (1.0 / det)
            slope = side * rtop
            g0 = jnp.where(row > m, cols[m] * rtop, 0.0)
            nxt = cols[m + 1] - g0 * side
            g1 = jnp.where(row > m + 1, nxt * rlow, 0.0)
            for q in range(m + 2, panel):
                u = cols[q][m:m + 1]
                v = cols[q][m + 1:m + 2] - slope * u
                cols[q] = (cols[q] - g0 * u) - g1 * v
            tile = tile - g0[:panel] * tile[m:m + 1]
            tile = tile - g1[:panel] * tile[m + 1:m + 2]
            pivots = jnp.where(row[:panel] == m, top, jnp.where(row[:panel] == m + 1, det * rtop, pivots))
            gains += [g0, g1]
        done.append(tile * lax.rsqrt(pivots))
        if height > panel:
            rest = rest[panel:]
            for m in range(panel):
                rest = rest - gains[m][panel:] * tile[m:m + 1]
    return jnp.concatenate(done, axis=0)


def inverse_factor_kernel(size, panel, mine_ref, out_ref, a_ref, y_ref):
    n = out_ref.shape[0]
    pieces, height, _ = mine_ref.shape
    r = lax.broadcasted_iota(jnp.int32, (n, n), 0)
    c = lax.broadcasted_iota(jnp.int32, (n, n), 1)
    gram = mine_ref[:, height - n // pieces:, :].reshape(n, n)
    diagonal = jnp.where(r == c, gram, 0.0)
    across = lax.rsqrt(jnp.sum(diagonal, axis=0, keepdims=True))
    down = lax.rsqrt(jnp.sum(diagonal, axis=1, keepdims=True))
    a_ref[...] = gram * across * down
    y_ref[...] = jnp.where(r == c, across, 0.0)
    count = n // size
    a = {}
    for i in range(count):
        for j in range(i + 1):
            a[i, j] = a_ref[i * size:(i + 1) * size, j * size:(j + 1) * size]
    eye = jnp.where(r[:size, :size] == c[:size, :size], 1.0, 0.0)
    y = [y_ref[i * size:(i + 1) * size, :] for i in range(count)]
    for k in range(count):
        small = factor_block(jnp.concatenate([a[k, k], eye], axis=1), panel)
        inverse = small[:, size:2 * size]
        p = {}
        for i in range(k + 1, count):
            p[i] = nt(a[i, k], inverse)
            for j in range(k + 1, i + 1):
                a[i, j] = a[i, j] - nt(p[i], p[j])
        lim = ((k + 1) * size + 127) // 128 * 128
        value = nn(inverse, y[k][:, :lim])
        out_ref[k * size:(k + 1) * size, :lim] = value
        if lim < n:
            out_ref[k * size:(k + 1) * size, lim:] = jnp.zeros((size, n - lim), jnp.float32)
        for i in range(k + 1, count):
            left = y[i][:, :lim] - nn(p[i], value)
            y[i] = left if lim == n else jnp.concatenate([left, y[i][:, lim:]], axis=1)


def inverse_factor(mine, size=64, panel=16):
    n = mine.shape[2]
    return pl.pallas_call(
        functools.partial(inverse_factor_kernel, size, panel),
        out_shape=jax.ShapeDtypeStruct((n, n), jnp.float32),
        in_specs=[VMEM],
        out_specs=VMEM,
        scratch_shapes=[pltpu.VMEM((n, n), jnp.float32), pltpu.VMEM((n, n), jnp.float32)],
        compiler_params=pltpu.CompilerParams(vmem_limit_bytes=8 * 1024 * 1024),
        name="inverse_factor",
    )(mine)


def sum_copies_kernel(in_ref, out_ref):
    count = in_ref.shape[0]
    total = in_ref[0]
    for index in range(1, count):
        total = total + in_ref[index]
    for index in range(count):
        out_ref[index] = total


def sum_copies(parts):
    return pl.pallas_call(
        sum_copies_kernel,
        out_shape=jax.ShapeDtypeStruct(parts.shape, parts.dtype),
        in_specs=[VMEM],
        out_specs=VMEM,
        compiler_params=pltpu.CompilerParams(vmem_limit_bytes=8 * 1024 * 1024),
        name="sum_copies",
    )(parts)


def right_kernel(mine_ref, inverse_ref, right_ref, sums_ref):
    pieces, height, rank = mine_ref.shape
    large = right_ref.shape[0] // pieces
    rows = mine_ref[:, :large, :].reshape(pieces * large, rank)
    right = nt(rows, inverse_ref[...])
    right_ref[...] = right
    sums_ref[...] = jnp.broadcast_to(jnp.sum(right * right, axis=0)[None, None], sums_ref.shape)


def right_and_sums(mine, inverse, count):
    pieces, height, rank = mine.shape
    large = height - rank // pieces
    return pl.pallas_call(
        right_kernel,
        out_shape=(
            jax.ShapeDtypeStruct((pieces * large, rank), jnp.float32),
            jax.ShapeDtypeStruct((count, 1, rank), jnp.float32),
        ),
        in_specs=[VMEM, VMEM],
        out_specs=(VMEM, VMEM),
        compiler_params=pltpu.CompilerParams(vmem_limit_bytes=10 * 1024 * 1024),
        name="right_and_sums",
    )(mine, inverse)


def sum_pair_kernel(mine_ref, other_ref, out_ref):
    out_ref[...] = mine_ref[...] + other_ref[...]


def sum_pair(mine, other):
    return pl.pallas_call(
        sum_pair_kernel,
        out_shape=jax.ShapeDtypeStruct(mine.shape, mine.dtype),
        in_specs=[VMEM, VMEM],
        out_specs=VMEM,
        compiler_params=pltpu.CompilerParams(vmem_limit_bytes=8 * 1024 * 1024),
        name="sum_pair",
    )(mine, other)


def feedback_kernel(left_ref, inverse_ref, mine_ref, other_ref, blend_ref, momentum_ref, factor_ref):
    factor = nt(left_ref[...], inverse_ref[...])
    factor_ref[...] = factor
    ortho = factor.astype(jnp.bfloat16)
    half = mine_ref.shape[0]
    for part in range(2):
        right = jnp.where(lax.axis_index("core") == part, mine_ref[...], other_ref[...])
        correction = lax.dot_general(
            ortho, right.astype(jnp.bfloat16), (((1,), (1,)), ((), ())), preferred_element_type=jnp.float32
        )
        at = part * half
        blend = blend_ref[:, at:at + half].astype(jnp.float32)
        momentum_ref[:, at:at + half] = (blend - 0.1 * correction).astype(jnp.bfloat16)


def feedback(left, inverse, mine, other, blend):
    return pl.pallas_call(
        feedback_kernel,
        out_shape=(jax.ShapeDtypeStruct(blend.shape, blend.dtype), jax.ShapeDtypeStruct(left.shape, jnp.float32)),
        in_specs=[VMEM] * 5,
        out_specs=(VMEM, VMEM),
        compiler_params=pltpu.CompilerParams(vmem_limit_bytes=12 * 1024 * 1024),
        cost_estimate=pl.CostEstimate(flops=0, bytes_accessed=0, transcendentals=0),
        name="feedback",
    )(left, inverse, mine, other, blend)


def normalize_kernel(mine_ref, other_ref, sums_ref, out_ref):
    scale = lax.rsqrt(jnp.sum(sums_ref[...], axis=0) + 1e-08)
    half = mine_ref.shape[0]
    for part in range(2):
        right = jnp.where(lax.axis_index("core") == part, mine_ref[...], other_ref[...])
        out_ref[part * half:(part + 1) * half, :] = (right * scale).astype(jnp.bfloat16)


def normalize(mine, other, sums):
    rows, rank = mine.shape
    return pl.pallas_call(
        normalize_kernel,
        out_shape=jax.ShapeDtypeStruct((2 * rows, rank), jnp.bfloat16),
        in_specs=[VMEM] * 3,
        out_specs=VMEM,
        compiler_params=pltpu.CompilerParams(vmem_limit_bytes=8 * 1024 * 1024),
        name="normalize",
    )(mine, other, sums)


def products_kernel(flip, left_ref, blend_ref, out_ref):
    left = left_ref[...]
    rank = left.shape[1]
    chips, height = out_ref.shape[:2]
    small = rank // chips
    large = height - small
    half = chips * large
    gram = lax.dot_general(left, left, (((0,), (0,)), ((), ())), precision=HIGHEST, preferred_element_type=jnp.float32)
    first = left.astype(jnp.bfloat16)
    rest = left - first.astype(jnp.float32)
    second = rest.astype(jnp.bfloat16)
    third = (rest - second.astype(jnp.float32)).astype(jnp.bfloat16)
    terms = jnp.concatenate([first, second, third], axis=1)
    part = 1 - lax.axis_index("core") if flip else lax.axis_index("core")
    both = lax.dot_general(
        blend_ref[:, pl.ds(pl.multiple_of(part * half, 128), half)], terms, (((0,), (0,)), ((), ())),
        preferred_element_type=jnp.float32,
    )
    product = both[:, :rank] + both[:, rank:2 * rank] + both[:, 2 * rank:]
    for chip in range(chips):
        out_ref[chip, :large, :] = product[chip * large:(chip + 1) * large]
        out_ref[chip, large:, :] = gram[chip * small:(chip + 1) * small]


def products(flip, left, blend, chips):
    rank = left.shape[1]
    height = blend.shape[1] // 2 // chips + rank // chips
    return pl.pallas_call(
        functools.partial(products_kernel, flip),
        out_shape=jax.ShapeDtypeStruct((chips, height, rank), jnp.float32),
        in_specs=[VMEM, VMEM],
        out_specs=VMEM,
        compiler_params=pltpu.CompilerParams(vmem_limit_bytes=12 * 1024 * 1024),
        name="products",
    )(left, blend)


def local(chips, cores, cols, momentum, gradient, right_factor):
    swap = [(0, 1), (1, 0)]
    blend = (momentum.astype(jnp.float32) + gradient.astype(jnp.float32)).astype(jnp.bfloat16)
    left = jnp.dot(blend, right_factor, preferred_element_type=jnp.float32)
    left = sum_copies(lax.all_to_all(left.reshape(cols, -1, left.shape[1]), "col", 0, 0))
    left = lax.all_to_all(left, "col", 0, 0).reshape(blend.shape[0], -1)
    other = lax.ppermute(products(True, left, blend, chips), "core", swap)
    both = sum_pair(products(False, left, blend, chips), other)
    mine = lax.all_to_all(sum_copies(lax.all_to_all(both, "chip", 0, 0)), "chip", 0, 0)
    inverse = inverse_factor(mine)
    right, sums = right_and_sums(mine, inverse, cores * cols)
    sums = lax.all_to_all(sums, ("core", "col"), 0, 0)
    other = lax.ppermute(right, "core", swap)
    new_momentum, left_factor = feedback(left, inverse, right, other, blend)
    new_right = normalize(right, other, sums)
    return (new_momentum, new_right, left_factor)


def solution(mesh):
    rows, cols = mesh.devices.shape
    chips, cores = rows // 2, 2
    split = Mesh(mesh.devices.reshape(chips, cores, cols), ("chip", "core", "col"))
    row = ("chip", "core")
    placed = (P(row, "col"), P(row, "col"), P("col", None))
    return jax.shard_map(
        functools.partial(local, chips, cores, cols),
        mesh=split,
        in_specs=placed,
        out_specs=(P(row, "col"), P("col", None), P(row, None)),
        check_vma=False,
    )
```

```python
import functools
import jax
import jax.numpy as jnp
from jax import lax
from jax.experimental import pallas as pl
from jax.experimental.pallas import tpu as pltpu
from jax.sharding import Mesh, PartitionSpec as P

HIGHEST = lax.Precision.HIGHEST
VMEM = pl.BlockSpec(memory_space=pltpu.VMEM)


def blend_of(momentum, gradient):
    return (momentum.astype(jnp.float32) + gradient.astype(jnp.float32)).astype(jnp.bfloat16)


def nt(a, b):
    return lax.dot_general(a, b, (((1,), (1,)), ((), ())), precision=HIGHEST, preferred_element_type=jnp.float32)


def nn(a, b):
    return lax.dot_general(a, b, (((1,), (0,)), ((), ())), precision=HIGHEST, preferred_element_type=jnp.float32)


def factor_block(block, panel):
    size = block.shape[0]
    rest = block
    done = []
    for start in range(0, size, panel):
        height = size - start
        row = lax.broadcasted_iota(jnp.int32, (height, 128), 0)
        cols = [jnp.broadcast_to(rest[:, start + m:start + m + 1], (height, 128)) for m in range(panel)]
        tile = rest[:panel]
        pivots = jnp.ones((panel, 128), jnp.float32)
        gains = []
        for m in range(0, panel, 2):
            top = cols[m][m:m + 1]
            side = cols[m + 1][m:m + 1]
            low = cols[m + 1][m + 1:m + 2]
            det = top * low - side * side
            rtop = 1.0 / top
            rlow = top * (1.0 / det)
            slope = side * rtop
            g0 = jnp.where(row > m, cols[m] * rtop, 0.0)
            nxt = cols[m + 1] - g0 * side
            g1 = jnp.where(row > m + 1, nxt * rlow, 0.0)
            for q in range(m + 2, panel):
                u = cols[q][m:m + 1]
                v = cols[q][m + 1:m + 2] - slope * u
                cols[q] = (cols[q] - g0 * u) - g1 * v
            tile = tile - g0[:panel] * tile[m:m + 1]
            tile = tile - g1[:panel] * tile[m + 1:m + 2]
            pivots = jnp.where(row[:panel] == m, top, jnp.where(row[:panel] == m + 1, det * rtop, pivots))
            gains += [g0, g1]
        done.append(tile * lax.rsqrt(pivots))
        if height > panel:
            rest = rest[panel:]
            for m in range(panel):
                rest = rest - gains[m][panel:] * tile[m:m + 1]
    return jnp.concatenate(done, axis=0)


def inverse_factor_kernel(size, panel, mine_ref, out_ref, a_ref, y_ref):
    n = out_ref.shape[0]
    pieces, height, _ = mine_ref.shape
    r = lax.broadcasted_iota(jnp.int32, (n, n), 0)
    c = lax.broadcasted_iota(jnp.int32, (n, n), 1)
    gram = mine_ref[:, height - n // pieces:, :].reshape(n, n)
    diagonal = jnp.where(r == c, gram, 0.0)
    across = lax.rsqrt(jnp.sum(diagonal, axis=0, keepdims=True))
    down = lax.rsqrt(jnp.sum(diagonal, axis=1, keepdims=True))
    a_ref[...] = gram * across * down
    y_ref[...] = jnp.where(r == c, across, 0.0)
    count = n // size
    a = {}
    for i in range(count):
        for j in range(i + 1):
            a[i, j] = a_ref[i * size:(i + 1) * size, j * size:(j + 1) * size]
    eye = jnp.where(r[:size, :size] == c[:size, :size], 1.0, 0.0)
    y = [y_ref[i * size:(i + 1) * size, :] for i in range(count)]
    for k in range(count):
        small = factor_block(jnp.concatenate([a[k, k], eye], axis=1), panel)
        inverse = small[:, size:2 * size]
        p = {}
        for i in range(k + 1, count):
            p[i] = nt(a[i, k], inverse)
            for j in range(k + 1, i + 1):
                a[i, j] = a[i, j] - nt(p[i], p[j])
        lim = ((k + 1) * size + 127) // 128 * 128
        value = nn(inverse, y[k][:, :lim])
        out_ref[k * size:(k + 1) * size, :lim] = value
        if lim < n:
            out_ref[k * size:(k + 1) * size, lim:] = jnp.zeros((size, n - lim), jnp.float32)
        for i in range(k + 1, count):
            left = y[i][:, :lim] - nn(p[i], value)
            y[i] = left if lim == n else jnp.concatenate([left, y[i][:, lim:]], axis=1)


def inverse_factor(mine, size=64, panel=16):
    n = mine.shape[2]
    return pl.pallas_call(
        functools.partial(inverse_factor_kernel, size, panel),
        out_shape=jax.ShapeDtypeStruct((n, n), jnp.float32),
        in_specs=[VMEM],
        out_specs=VMEM,
        scratch_shapes=[pltpu.VMEM((n, n), jnp.float32), pltpu.VMEM((n, n), jnp.float32)],
        compiler_params=pltpu.CompilerParams(vmem_limit_bytes=8 * 1024 * 1024),
        name="inverse_factor",
    )(mine)


def sum_copies_kernel(in_ref, out_ref):
    count = in_ref.shape[0]
    total = in_ref[0]
    for index in range(1, count):
        total = total + in_ref[index]
    for index in range(out_ref.shape[0]):
        out_ref[index] = total


def sum_copies(parts, count):
    return pl.pallas_call(
        sum_copies_kernel,
        out_shape=jax.ShapeDtypeStruct((count,) + parts.shape[1:], parts.dtype),
        in_specs=[VMEM],
        out_specs=VMEM,
        compiler_params=pltpu.CompilerParams(vmem_limit_bytes=8 * 1024 * 1024),
        name="sum_copies",
    )(parts)


def right_kernel(mine_ref, inverse_ref, first_ref, second_ref, sums_ref):
    pieces, height, rank = mine_ref.shape
    half = first_ref.shape[0]
    large = 2 * half // pieces
    rows = mine_ref[:, :large, :].reshape(pieces * large, rank)
    right = nt(rows, inverse_ref[...])
    first_ref[...] = right[:half]
    second_ref[...] = right[half:]
    sums_ref[...] = jnp.broadcast_to(jnp.sum(right * right, axis=0)[None, None], sums_ref.shape)


def right_and_sums(mine, inverse, count):
    pieces, height, rank = mine.shape
    part = jax.ShapeDtypeStruct((pieces * (height - rank // pieces) // 2, rank), jnp.float32)
    return pl.pallas_call(
        right_kernel,
        out_shape=(part, part, jax.ShapeDtypeStruct((count, 1, rank), jnp.float32)),
        in_specs=[VMEM, VMEM],
        out_specs=(VMEM, VMEM, VMEM),
        compiler_params=pltpu.CompilerParams(vmem_limit_bytes=10 * 1024 * 1024),
        name="right_and_sums",
    )(mine, inverse)


def sum_pair_kernel(mine_ref, other_ref, out_ref):
    out_ref[...] = mine_ref[...] + other_ref[...]


def sum_pair(mine, other):
    return pl.pallas_call(
        sum_pair_kernel,
        out_shape=jax.ShapeDtypeStruct(mine.shape, mine.dtype),
        in_specs=[VMEM, VMEM],
        out_specs=VMEM,
        compiler_params=pltpu.CompilerParams(vmem_limit_bytes=8 * 1024 * 1024),
        name="sum_pair",
    )(mine, other)


def feedback_kernel(left_ref, inverse_ref, first_ref, second_ref, old_ref, gradient_ref, new_ref, factor_ref):
    factor = nt(left_ref[...], inverse_ref[...])
    factor_ref[...] = factor
    ortho = factor.astype(jnp.bfloat16)
    cores = first_ref.shape[0]
    half = old_ref.shape[1] // cores
    for core in range(cores):
        right = jnp.concatenate([first_ref[core], second_ref[core]], axis=0)
        correction = lax.dot_general(
            ortho, right.astype(jnp.bfloat16), (((1,), (1,)), ((), ())), preferred_element_type=jnp.float32
        )
        at = core * half
        blend = blend_of(old_ref[:, at:at + half], gradient_ref[:, at:at + half])
        new_ref[:, at:at + half] = (blend.astype(jnp.float32) - 0.1 * correction).astype(jnp.bfloat16)


def feedback(left, inverse, first, second, momentum, gradient):
    return pl.pallas_call(
        feedback_kernel,
        out_shape=(jax.ShapeDtypeStruct(momentum.shape, momentum.dtype), jax.ShapeDtypeStruct(left.shape, jnp.float32)),
        in_specs=[VMEM] * 6,
        out_specs=(VMEM, VMEM),
        compiler_params=pltpu.CompilerParams(vmem_limit_bytes=12 * 1024 * 1024),
        cost_estimate=pl.CostEstimate(flops=0, bytes_accessed=0, transcendentals=0),
        name="feedback",
    )(left, inverse, first, second, momentum, gradient)


def normalize_kernel(first_ref, second_ref, sums_ref, out_ref):
    scale = lax.rsqrt(jnp.sum(sums_ref[...], axis=0) + 1e-08)
    cores, part = first_ref.shape[:2]
    for core in range(cores):
        for index, source in enumerate((first_ref, second_ref)):
            at = (2 * core + index) * part
            out_ref[at:at + part, :] = (source[core] * scale).astype(jnp.bfloat16)


def normalize(first, second, sums):
    cores, part, rank = first.shape
    return pl.pallas_call(
        normalize_kernel,
        out_shape=jax.ShapeDtypeStruct((2 * cores * part, rank), jnp.bfloat16),
        in_specs=[VMEM] * 3,
        out_specs=VMEM,
        compiler_params=pltpu.CompilerParams(vmem_limit_bytes=8 * 1024 * 1024),
        name="normalize",
    )(first, second, sums)


def products_kernel(flip, left_ref, blend_ref, out_ref):
    left = left_ref[...]
    rank = left.shape[1]
    chips, height = out_ref.shape[:2]
    small = rank // chips
    large = height - small
    half = chips * large
    gram = lax.dot_general(left, left, (((0,), (0,)), ((), ())), precision=HIGHEST, preferred_element_type=jnp.float32)
    first = left.astype(jnp.bfloat16)
    rest = left - first.astype(jnp.float32)
    second = rest.astype(jnp.bfloat16)
    third = (rest - second.astype(jnp.float32)).astype(jnp.bfloat16)
    terms = jnp.concatenate([first, second, third], axis=1)
    part = 1 - lax.axis_index("core") if flip else lax.axis_index("core")
    both = lax.dot_general(
        blend_ref[:, pl.ds(pl.multiple_of(part * half, 128), half)], terms, (((0,), (0,)), ((), ())),
        preferred_element_type=jnp.float32,
    )
    product = both[:, :rank] + both[:, rank:2 * rank] + both[:, 2 * rank:]
    for chip in range(chips):
        out_ref[chip, :large, :] = product[chip * large:(chip + 1) * large]
        out_ref[chip, large:, :] = gram[chip * small:(chip + 1) * small]


def products(flip, left, blend, chips):
    rank = left.shape[1]
    height = blend.shape[1] // 2 // chips + rank // chips
    return pl.pallas_call(
        functools.partial(products_kernel, flip),
        out_shape=jax.ShapeDtypeStruct((chips, height, rank), jnp.float32),
        in_specs=[VMEM, VMEM],
        out_specs=VMEM,
        compiler_params=pltpu.CompilerParams(vmem_limit_bytes=12 * 1024 * 1024),
        name="products",
    )(left, blend)


def local(chips, cores, cols, momentum, gradient, right_factor):
    swap = [(0, 1), (1, 0)]
    blend = blend_of(momentum, gradient)
    left = jnp.dot(blend, right_factor, preferred_element_type=jnp.float32)
    left = sum_copies(lax.all_to_all(left.reshape(cols, -1, left.shape[1]), ("near", "far"), 0, 0), cols // 2)
    left = lax.all_to_all(left, "far", 0, 0).reshape(blend.shape[0] // 2, -1)
    left = lax.all_gather(left, "near", tiled=True)
    other = lax.ppermute(products(True, left, blend, chips), "core", swap)
    both = sum_pair(products(False, left, blend, chips), other)
    mine = lax.all_to_all(sum_copies(lax.all_to_all(both, "chip", 0, 0), chips), "chip", 0, 0)
    inverse = inverse_factor(mine)
    first, second, sums = right_and_sums(mine, inverse, cores * cols)
    sums = lax.all_to_all(sums, ("core", "far", "near"), 0, 0)
    first, second = lax.all_gather(first, "core"), lax.all_gather(second, "core")
    new_momentum, left_factor = feedback(left, inverse, first, second, momentum, gradient)
    new_right = normalize(first, second, sums)
    return (new_momentum, new_right, left_factor)


def solution(mesh):
    rows, cols = mesh.devices.shape
    chips, cores = rows // 2, 2
    split = Mesh(mesh.devices.reshape(chips, cores, cols // 2, 2), ("chip", "core", "far", "near"))
    col = ("far", "near")
    row = ("chip", "core")
    placed = (P(row, col), P(row, col), P(col, None))
    return jax.shard_map(
        functools.partial(local, chips, cores, cols),
        mesh=split,
        in_specs=placed,
        out_specs=(P(row, col), P(col, None), P(row, None)),
        check_vma=False,
    )
```

```python
import functools
import jax
import jax.numpy as jnp
from jax import lax
from jax.experimental import pallas as pl
from jax.experimental.pallas import tpu as pltpu
from jax.sharding import Mesh, PartitionSpec as P

HIGHEST = lax.Precision.HIGHEST
VMEM = pl.BlockSpec(memory_space=pltpu.VMEM)


def blend_of(momentum, gradient):
    return (momentum.astype(jnp.float32) + gradient.astype(jnp.float32)).astype(jnp.bfloat16)


def nt(a, b):
    return lax.dot_general(a, b, (((1,), (1,)), ((), ())), precision=HIGHEST, preferred_element_type=jnp.float32)


def nn(a, b):
    return lax.dot_general(a, b, (((1,), (0,)), ((), ())), precision=HIGHEST, preferred_element_type=jnp.float32)


def factor_block(block, panel):
    size = block.shape[0]
    rest = block
    done = []
    for start in range(0, size, panel):
        height = size - start
        row = lax.broadcasted_iota(jnp.int32, (height, 128), 0)
        cols = [jnp.broadcast_to(rest[:, start + m:start + m + 1], (height, 128)) for m in range(panel)]
        tile = rest[:panel]
        pivots = jnp.ones((panel, 128), jnp.float32)
        gains = []
        for m in range(0, panel, 2):
            top = cols[m][m:m + 1]
            side = cols[m + 1][m:m + 1]
            low = cols[m + 1][m + 1:m + 2]
            det = top * low - side * side
            rtop = 1.0 / top
            rlow = top * (1.0 / det)
            slope = side * rtop
            g0 = jnp.where(row > m, cols[m] * rtop, 0.0)
            nxt = cols[m + 1] - g0 * side
            g1 = jnp.where(row > m + 1, nxt * rlow, 0.0)
            for q in range(m + 2, panel):
                u = cols[q][m:m + 1]
                v = cols[q][m + 1:m + 2] - slope * u
                cols[q] = (cols[q] - g0 * u) - g1 * v
            tile = tile - g0[:panel] * tile[m:m + 1]
            tile = tile - g1[:panel] * tile[m + 1:m + 2]
            pivots = jnp.where(row[:panel] == m, top, jnp.where(row[:panel] == m + 1, det * rtop, pivots))
            gains += [g0, g1]
        done.append(tile * lax.rsqrt(pivots))
        if height > panel:
            rest = rest[panel:]
            for m in range(panel):
                rest = rest - gains[m][panel:] * tile[m:m + 1]
    return jnp.concatenate(done, axis=0)


def inverse_factor_kernel(size, panel, gram_ref, out_ref, a_ref, y_ref):
    n = out_ref.shape[0]
    r = lax.broadcasted_iota(jnp.int32, (n, n), 0)
    c = lax.broadcasted_iota(jnp.int32, (n, n), 1)
    gram = gram_ref[...]
    diagonal = jnp.where(r == c, gram, 0.0)
    across = lax.rsqrt(jnp.sum(diagonal, axis=0, keepdims=True))
    down = lax.rsqrt(jnp.sum(diagonal, axis=1, keepdims=True))
    a_ref[...] = gram * across * down
    y_ref[...] = jnp.where(r == c, across, 0.0)
    count = n // size
    a = {}
    for i in range(count):
        for j in range(i + 1):
            a[i, j] = a_ref[i * size:(i + 1) * size, j * size:(j + 1) * size]
    eye = jnp.where(r[:size, :size] == c[:size, :size], 1.0, 0.0)
    y = [y_ref[i * size:(i + 1) * size, :] for i in range(count)]
    for k in range(count):
        small = factor_block(jnp.concatenate([a[k, k], eye], axis=1), panel)
        inverse = small[:, size:2 * size]
        p = {}
        for i in range(k + 1, count):
            p[i] = nt(a[i, k], inverse)
            for j in range(k + 1, i + 1):
                a[i, j] = a[i, j] - nt(p[i], p[j])
        lim = ((k + 1) * size + 127) // 128 * 128
        value = nn(inverse, y[k][:, :lim])
        out_ref[k * size:(k + 1) * size, :lim] = value
        if lim < n:
            out_ref[k * size:(k + 1) * size, lim:] = jnp.zeros((size, n - lim), jnp.float32)
        for i in range(k + 1, count):
            left = y[i][:, :lim] - nn(p[i], value)
            y[i] = left if lim == n else jnp.concatenate([left, y[i][:, lim:]], axis=1)


def inverse_factor(gram, size=64, panel=16):
    n = gram.shape[0]
    return pl.pallas_call(
        functools.partial(inverse_factor_kernel, size, panel),
        out_shape=jax.ShapeDtypeStruct((n, n), jnp.float32),
        in_specs=[VMEM],
        out_specs=VMEM,
        scratch_shapes=[pltpu.VMEM((n, n), jnp.float32), pltpu.VMEM((n, n), jnp.float32)],
        compiler_params=pltpu.CompilerParams(vmem_limit_bytes=8 * 1024 * 1024),
        name="inverse_factor",
    )(gram)


def sum_copies_kernel(in_ref, out_ref):
    count = in_ref.shape[0]
    total = in_ref[0]
    for index in range(1, count):
        total = total + in_ref[index]
    for index in range(out_ref.shape[0]):
        out_ref[index] = total


def sum_copies(parts, count):
    return pl.pallas_call(
        sum_copies_kernel,
        out_shape=jax.ShapeDtypeStruct((count,) + parts.shape[1:], parts.dtype),
        in_specs=[VMEM],
        out_specs=VMEM,
        compiler_params=pltpu.CompilerParams(vmem_limit_bytes=8 * 1024 * 1024),
        name="sum_copies",
    )(parts)


def right_kernel(mine_ref, inverse_ref, first_ref, second_ref, sums_ref):
    pieces, height, rank = mine_ref.shape
    half = first_ref.shape[0]
    large = 2 * half // pieces
    rows = mine_ref[:, :large, :].reshape(pieces * large, rank)
    right = nt(rows, inverse_ref[...])
    first_ref[...] = right[:half]
    second_ref[...] = right[half:]
    sums_ref[...] = jnp.broadcast_to(jnp.sum(right * right, axis=0)[None, None], sums_ref.shape)


def right_and_sums(mine, inverse, count):
    pieces, height, rank = mine.shape
    part = jax.ShapeDtypeStruct((pieces * (height - rank // 2 // pieces) // 2, rank), jnp.float32)
    return pl.pallas_call(
        right_kernel,
        out_shape=(part, part, jax.ShapeDtypeStruct((count, 1, rank), jnp.float32)),
        in_specs=[VMEM, VMEM],
        out_specs=(VMEM, VMEM, VMEM),
        compiler_params=pltpu.CompilerParams(vmem_limit_bytes=10 * 1024 * 1024),
        name="right_and_sums",
    )(mine, inverse)


def sum_pair_kernel(mine_ref, other_ref, out_ref):
    out_ref[...] = mine_ref[...] + other_ref[...]


def sum_pair(mine, other):
    return pl.pallas_call(
        sum_pair_kernel,
        out_shape=jax.ShapeDtypeStruct(mine.shape, mine.dtype),
        in_specs=[VMEM, VMEM],
        out_specs=VMEM,
        compiler_params=pltpu.CompilerParams(vmem_limit_bytes=8 * 1024 * 1024),
        name="sum_pair",
    )(mine, other)


def feedback_kernel(left_ref, inverse_ref, first_ref, second_ref, old_ref, gradient_ref, new_ref, factor_ref):
    factor = nt(left_ref[...], inverse_ref[...])
    factor_ref[...] = factor
    ortho = factor.astype(jnp.bfloat16)
    cores = first_ref.shape[0]
    half = old_ref.shape[1] // cores
    for core in range(cores):
        right = jnp.concatenate([first_ref[core], second_ref[core]], axis=0)
        correction = lax.dot_general(
            ortho, right.astype(jnp.bfloat16), (((1,), (1,)), ((), ())), preferred_element_type=jnp.float32
        )
        at = core * half
        blend = blend_of(old_ref[:, at:at + half], gradient_ref[:, at:at + half])
        new_ref[:, at:at + half] = (blend.astype(jnp.float32) - 0.1 * correction).astype(jnp.bfloat16)


def feedback(left, inverse, first, second, momentum, gradient):
    return pl.pallas_call(
        feedback_kernel,
        out_shape=(jax.ShapeDtypeStruct(momentum.shape, momentum.dtype), jax.ShapeDtypeStruct(left.shape, jnp.float32)),
        in_specs=[VMEM] * 6,
        out_specs=(VMEM, VMEM),
        compiler_params=pltpu.CompilerParams(vmem_limit_bytes=12 * 1024 * 1024),
        cost_estimate=pl.CostEstimate(flops=0, bytes_accessed=0, transcendentals=0),
        name="feedback",
    )(left, inverse, first, second, momentum, gradient)


def normalize_kernel(first_ref, second_ref, sums_ref, out_ref):
    scale = lax.rsqrt(jnp.sum(sums_ref[...], axis=0) + 1e-08)
    cores, part = first_ref.shape[:2]
    for core in range(cores):
        for index, source in enumerate((first_ref, second_ref)):
            at = (2 * core + index) * part
            out_ref[at:at + part, :] = (source[core] * scale).astype(jnp.bfloat16)


def normalize(first, second, sums):
    cores, part, rank = first.shape
    return pl.pallas_call(
        normalize_kernel,
        out_shape=jax.ShapeDtypeStruct((2 * cores * part, rank), jnp.bfloat16),
        in_specs=[VMEM] * 3,
        out_specs=VMEM,
        compiler_params=pltpu.CompilerParams(vmem_limit_bytes=8 * 1024 * 1024),
        name="normalize",
    )(first, second, sums)


def products_kernel(flip, left_ref, blend_ref, out_ref):
    left = left_ref[...]
    rank = left.shape[1]
    chips, height = out_ref.shape[:2]
    small = rank // 2 // chips
    large = height - small
    half = chips * large
    first = left.astype(jnp.bfloat16)
    rest = left - first.astype(jnp.float32)
    second = rest.astype(jnp.bfloat16)
    third = (rest - second.astype(jnp.float32)).astype(jnp.bfloat16)
    terms = jnp.concatenate([first, second, third], axis=1)
    part = 1 - lax.axis_index("core") if flip else lax.axis_index("core")
    columns = left_ref[:, pl.ds(pl.multiple_of(part * (rank // 2), 128), rank // 2)]
    gram = lax.dot_general(columns, left, (((0,), (0,)), ((), ())), precision=HIGHEST, preferred_element_type=jnp.float32)
    both = lax.dot_general(
        blend_ref[:, pl.ds(pl.multiple_of(part * half, 128), half)], terms, (((0,), (0,)), ((), ())),
        preferred_element_type=jnp.float32,
    )
    product = both[:, :rank] + both[:, rank:2 * rank] + both[:, 2 * rank:]
    for chip in range(chips):
        out_ref[chip, :large, :] = product[chip * large:(chip + 1) * large]
        out_ref[chip, large:, :] = gram[chip * small:(chip + 1) * small]


def products(flip, left, blend, chips):
    rank = left.shape[1]
    height = blend.shape[1] // 2 // chips + rank // 2 // chips
    return pl.pallas_call(
        functools.partial(products_kernel, flip),
        out_shape=jax.ShapeDtypeStruct((chips, height, rank), jnp.float32),
        in_specs=[VMEM, VMEM],
        out_specs=VMEM,
        compiler_params=pltpu.CompilerParams(vmem_limit_bytes=12 * 1024 * 1024),
        name="products",
    )(left, blend)


def local(chips, cores, cols, momentum, gradient, right_factor):
    swap = [(0, 1), (1, 0)]
    blend = blend_of(momentum, gradient)
    left = jnp.dot(blend, right_factor, preferred_element_type=jnp.float32)
    left = sum_copies(lax.all_to_all(left.reshape(cols, -1, left.shape[1]), ("near", "far"), 0, 0), cols // 2)
    left = lax.all_to_all(left, "far", 0, 0).reshape(blend.shape[0] // 2, -1)
    left = lax.all_gather(left, "near", tiled=True)
    other = lax.ppermute(products(True, left, blend, chips), "core", swap)
    both = sum_pair(products(False, left, blend, chips), other)
    mine = lax.all_to_all(sum_copies(lax.all_to_all(both, "chip", 0, 0), chips), "chip", 0, 0)
    rank = mine.shape[2]
    gram = mine[:, mine.shape[1] - rank // 2 // chips:, :].reshape(rank // 2, rank)
    inverse = inverse_factor(lax.all_gather(gram, "core", tiled=True))
    first, second, sums = right_and_sums(mine, inverse, cores * cols)
    sums = lax.all_to_all(sums, ("core", "far", "near"), 0, 0)
    first, second = lax.all_gather(first, "core"), lax.all_gather(second, "core")
    new_momentum, left_factor = feedback(left, inverse, first, second, momentum, gradient)
    new_right = normalize(first, second, sums)
    return (new_momentum, new_right, left_factor)


def solution(mesh):
    rows, cols = mesh.devices.shape
    chips, cores = rows // 2, 2
    split = Mesh(mesh.devices.reshape(chips, cores, cols // 2, 2), ("chip", "core", "far", "near"))
    col = ("far", "near")
    row = ("chip", "core")
    placed = (P(row, col), P(row, col), P(col, None))
    return jax.shard_map(
        functools.partial(local, chips, cores, cols),
        mesh=split,
        in_specs=placed,
        out_specs=(P(row, col), P(col, None), P(row, None)),
        check_vma=False,
    )
```
